1024 devices in a mesh: pair: 64 (over y, z_lo, core), virt: 16 (over z_hi, x).
Axes of the slice: x: 8, y: 8, z: 8 (z_hi: 2, z_lo: 4; z = z_hi * 4 + z_lo), core: 2. Of those that a mesh axis runs over, the one named last changes fastest.
Arguments:
- amplitudes: bfloat16 [384, 16, 128, 2048], P('pair', None, None, 'virt'), may hold values from -6 to 6
- integrals: bfloat16 [128, 2048, 128], P('pair', 'virt'), may hold values from -0.03125 to 0.03125
- tile_blocks: int32 [384, 2], P('pair'), may hold values from 0 to 31, as said below
- occ_irrep: int32 [128], replicated, may hold values from 0 to 7
- slab_irrep: int32 [128], replicated, may hold values from 0 to 7
- virt_irrep: int32 [2048], P('virt'), may hold values from 0 to 7
- ab_irrep: int32 [128], replicated, may hold values from 0 to 7
- occ_energy: float32 [128], replicated, may hold values from -2 to -0.5
- ab_energy: float32 [128], replicated, may hold values from 0.5 to 4
Outputs:
- update: float32 [384, 16, 128], P('pair')
The draws below stay inside these ranges and needn't reach their ends.
Inputs may be any that keep to these rules, and one draw needn't show every extreme that they name: `tile_blocks`: each row is two different blocks; with H = 32, the tile at position t * 6 + s holds the blocks of the tile at ((t + H) % (2 * H)) * 6 + s in reverse order.
All inputs are finite; a program needn't handle non-finite values.
Results may differ from the reference program's by a relative error of at most 0.0003.
Values may be sent and summed in bfloat16 or wider, within the bound.
A program may use at most 32 MiB of HBM per device.

```python
import jax
import jax.numpy as jnp
from jax import lax

OB = 4
NBLK = 32
NOCC = 128
VIRT = 2048
SLAB = 128
AB = 128
TILES_DEV = 6
TILES = 384
N_PAIR = 64


def draw_tile_blocks(key, part):
    key = jax.random.fold_in(key, 11)
    key_first, key_step = jax.random.split(key)
    half = N_PAIR // 2
    first = jax.random.randint(key_first, (half, TILES_DEV), 0, NBLK)
    step = jax.random.randint(key_step, (half, TILES_DEV), 1, NBLK)
    second = (first + step) % NBLK
    upper = jnp.stack([first, second], -1)
    lower = jnp.stack([second, first], -1)
    return jnp.concatenate([upper, lower], 0).reshape(N_PAIR * TILES_DEV, 2).astype(jnp.int32)


def with_ends(result, rng, smallest, largest):
    place = [jax.random.randint(jax.random.fold_in(rng, axis), (), 0, length) for axis, length in enumerate(result.shape)]
    widest = result.shape.index(max(result.shape))
    next_to = place[:widest] + [(place[widest] + 1) % result.shape[widest]] + place[widest + 1:]
    return result.at[tuple(place)].set(smallest).at[tuple(next_to)].set(largest)


def block_levels(stream_key, dims, pieces, low, high):
    factor_of = 1.0
    for dim, blocks in pieces:
        draws = jax.random.uniform(jax.random.fold_in(jax.random.fold_in(stream_key, 6), dim), (blocks,), jnp.float32, low / len(pieces), high / len(pieces))
        factor_of = factor_of * jnp.repeat(jnp.exp(draws), dims[dim] // blocks).reshape((-1,) + (1,) * (len(dims) - 1 - dim))
    return factor_of


def centred(own_key, extent, scale, reach, pieces=(), held_as=jnp.bfloat16):
    level = block_levels(own_key, extent, pieces, -0.22, 0.18) if pieces else 1.0
    drawn = jax.random.normal(own_key, extent, jnp.float32) * scale * level
    return jnp.minimum(jnp.maximum(drawn, -reach), reach).astype(held_as)


def setup_inputs(seed: int = 0) -> dict:
    seeds = jax.random.split(jax.random.key(seed), 10)
    amplitudes = centred(seeds[0], (TILES, OB * OB, SLAB, VIRT), 1.0, 6.0, ((0, 64), (3, 16)))
    integrals = centred(seeds[1], (SLAB, VIRT, AB), (SLAB * VIRT // 8) ** -0.5, 0.03125, ((0, 64), (1, 16)))
    tile_blocks = draw_tile_blocks(jax.random.fold_in(seeds[9], 71), 0)
    occ_irrep = with_ends(jax.random.randint(seeds[3], (NOCC,), 0, 8), jax.random.fold_in(seeds[3], 1), 0, 7).astype(jnp.int32)
    slab_irrep = with_ends(jax.random.randint(seeds[4], (SLAB,), 0, 8), jax.random.fold_in(seeds[4], 1), 0, 7).astype(jnp.int32)
    virt_irrep = with_ends(jax.random.randint(seeds[5], (VIRT,), 0, 8), jax.random.fold_in(seeds[5], 1), 0, 7).astype(jnp.int32)
    ab_irrep = with_ends(jax.random.randint(seeds[6], (AB,), 0, 8), jax.random.fold_in(seeds[6], 1), 0, 7).astype(jnp.int32)
    occ_energy = jnp.clip(jax.random.uniform(seeds[7], (NOCC,), jnp.float32, -2.0, -0.5), -2.0, -0.5)
    ab_energy = jnp.clip(jax.random.uniform(seeds[8], (AB,), jnp.float32, 0.5, 4.0), 0.5, 4.0)
    return dict(amplitudes=amplitudes, integrals=integrals, tile_blocks=tile_blocks, occ_irrep=occ_irrep, slab_irrep=slab_irrep, virt_irrep=virt_irrep, ab_irrep=ab_irrep, occ_energy=occ_energy, ab_energy=ab_energy)


def reference(amplitudes, integrals, tile_blocks, occ_irrep, slab_irrep, virt_irrep, ab_irrep, occ_energy, ab_energy):
    local = jnp.arange(OB * OB, dtype=jnp.int32)
    first = local // OB
    second = local % OB
    occ_i = tile_blocks[:, 0:1] * OB + first[None, :]
    occ_j = tile_blocks[:, 1:2] * OB + second[None, :]
    pair_irrep = jnp.bitwise_xor(occ_irrep[occ_i], occ_irrep[occ_j])
    flat = integrals.reshape(SLAB * VIRT, AB)
    cd_irrep = jnp.bitwise_xor(slab_irrep[:, None], virt_irrep[None, :])

    def one_tile(item):
        amps, irrep = item
        keep = jnp.bitwise_xor(irrep[:, None, None], cd_irrep[None]) == 0
        masked = jnp.where(keep, amps, jnp.zeros((), amps.dtype))
        return jnp.dot(masked.reshape(OB * OB, SLAB * VIRT), flat, preferred_element_type=jnp.float32)

    ladder = lax.map(one_tile, (amplitudes, pair_irrep))
    grid = ladder.reshape(N_PAIR, TILES_DEV, OB, OB, AB)
    mirror = jnp.swapaxes(jnp.roll(grid, N_PAIR // 2, axis=0), 2, 3).reshape(TILES, OB * OB, AB)
    combined = 0.5 * (ladder - mirror)
    denom = (occ_energy[occ_i] + occ_energy[occ_j])[:, :, None] - ab_energy[None, None, :]
    keep = jnp.bitwise_xor(pair_irrep[:, :, None], ab_irrep[None, None, :]) == 0
    return jnp.where(keep, combined / denom, jnp.zeros((), combined.dtype))
```

```python
import functools

import jax
import jax.numpy as jnp
from jax import lax
from jax.experimental import pallas as pl
from jax.experimental.pallas import tpu as pltpu
from jax.sharding import PartitionSpec as P

OB = 4
TILES = 6
ROWS = TILES * OB * OB
LANES = 128
WIDTH = 32
HALF = WIDTH // 2
NY, NZ, NCORE, NX, NH = 8, 4, 2, 8, 2
PITCH = 136
MESH = pl.DeviceIdType.MESH
NT = (((1,), (1,)), ((), ()))
TN = (((0,), (0,)), ((), ()))


def place():
    pair, virt = lax.axis_index("pair"), lax.axis_index("virt")
    return pair // (NZ * NCORE), (pair // NCORE) % NZ, pair % NCORE, virt // NX, virt % NX


def kernel(
    tile_blocks, occ_irrep, slab_scalar, occ_energy, chunk, amps, ints, virt, slab, ab, ab_energy,
    out, top,
    held, spread, rows, lo, hi, factor, over_x, over_m, result, sem_in, send, recv,
):
    y, z, core, half, x = place()
    mirror = y // (NY // 2)

    def at(dy=0, dz=0, dc=0, dh=0, dx=0):
        pair = ((y + dy) % NY) * (NZ * NCORE) + ((z + dz) % NZ) * NCORE + (core + dc) % NCORE
        return pair, ((half + dh) % NH) * NX + (x + dx) % NX

    peers = [at(dy=k) for k in range(1, NY)] + [at(dz=k) for k in range(1, NZ)] + [at(dc=1)]
    peers += [at(dx=k) for k in range(1, NX)] + [at(dh=1), at(dy=NY // 2, dh=1)]
    barrier = pltpu.get_barrier_semaphore()
    for peer in peers:
        pl.semaphore_signal(barrier, inc=1, device_id=peer, device_id_type=MESH)

    load = pltpu.make_async_copy(amps, held, sem_in)
    load.start()

    def remote(src, dst, number, peer):
        return pltpu.make_async_remote_copy(
            src_ref=src, dst_ref=dst, send_sem=send.at[number], recv_sem=recv.at[number],
            device_id=peer, device_id_type=MESH,
        )

    ab_row = ab[...]
    ab_rows = jnp.broadcast_to(ab_row, (LANES, LANES))
    ab_cols = jnp.transpose(ab_rows)
    before = lax.broadcasted_iota(jnp.int32, (LANES, LANES), 0) < lax.broadcasted_iota(jnp.int32, (LANES, LANES), 1)
    same = jnp.where((ab_rows == ab_cols) & before, 1.0, 0.0)
    rank = jnp.sum(same, axis=0, keepdims=True).astype(jnp.int32)
    top[...] = jnp.broadcast_to(jnp.max(rank, axis=1, keepdims=True), top.shape)
    slot = lax.broadcasted_iota(jnp.int32, (WIDTH, LANES), 0) + chunk[0] * WIDTH
    pick = jnp.where(slot == jnp.broadcast_to(rank, (WIDTH, LANES)), 1.0, 0.0)
    pick_narrow = pick.astype(jnp.bfloat16)
    virt_rows = jnp.broadcast_to(virt[...], (LANES, LANES))
    virt_cols = jnp.transpose(virt_rows)
    labels = jnp.bitwise_xor(virt_cols, ab_rows)
    own = (y * NZ + z) * NCORE + core
    for c in range(2):
        kept = jnp.where(labels == slab_scalar[own * 2 + c], ints[c].astype(jnp.float32), 0.0).astype(jnp.bfloat16)
        packed = lax.dot_general(pick_narrow, kept, NT, preferred_element_type=jnp.float32).astype(jnp.bfloat16)
        lo[core, y, z, :, c * LANES:(c + 1) * LANES] = packed[:HALF]
        hi[core, z, y, :, c * LANES:(c + 1) * LANES] = packed[HALF:]

    pl.semaphore_wait(barrier, len(peers))

    sends = []
    n = 0
    first = []
    for k in range(1, NZ):
        copy = remote(lo.at[core, y, z], lo.at[core, y, z], n, at(dz=k))
        copy.start()
        sends.append(copy)
        first.append(remote(lo.at[core, y, z], lo.at[core, y, (z - k + NZ) % NZ], n, at(dz=k)))
        n += 1
    for k in range(1, NY):
        copy = remote(hi.at[core, z, y], hi.at[core, z, y], n, at(dy=k))
        copy.start()
        sends.append(copy)
        first.append(remote(hi.at[core, z, y], hi.at[core, z, (y - k + NY) % NY], n, at(dy=k)))
        n += 1

    load.wait()
    cd = jnp.bitwise_xor(jnp.transpose(jnp.broadcast_to(slab[...], (LANES, LANES))), virt_rows)
    sign = (1 - 2 * mirror).astype(jnp.float32)

    def mask_tile(k, carry):
        for q in range(OB * OB):
            i, j = q // OB, q % OB
            source = k * (OB * OB) + q + mirror * (j * OB + i - q)
            a = tile_blocks[k, 0] * OB + (i + mirror * (j - i))
            b = tile_blocks[k, 1] * OB + (j + mirror * (i - j))
            irrep = jnp.bitwise_xor(occ_irrep[a], occ_irrep[b])
            energy = occ_energy[a] + occ_energy[b]
            row = k * (OB * OB) + q
            spread[pl.ds(pl.multiple_of(row * PITCH, 8), LANES), :] = jnp.where(
                cd == irrep, held[source].astype(jnp.float32), 0.0
            )
            factor[pl.ds(row, 1), :] = jnp.where(ab_row == irrep, sign / (energy - ab_energy[...]), 0.0)
        return carry

    lax.fori_loop(0, TILES, mask_tile, 0)

    for copy in first:
        copy.wait_recv()

    second_lo, second_hi = [], []
    for k in range(1, NY):
        copy = remote(lo.at[core, y], lo.at[core, y], n, at(dy=k))
        copy.start()
        sends.append(copy)
        second_lo.append(((y - k + NY) % NY, n, at(dy=k)))
        n += 1
    for k in range(1, NZ):
        copy = remote(hi.at[core, z], hi.at[core, z], n, at(dz=k))
        copy.start()
        sends.append(copy)
        second_hi.append(((z - k + NZ) % NZ, n, at(dz=k)))
        n += 1

    forwards = []

    def forward(ref, index):
        nonlocal n
        copy = remote(ref.at[core, index], ref.at[core, index], n, at(dc=1))
        copy.start()
        sends.append(copy)
        forwards.append(remote(ref.at[core, index], ref.at[1 - core, index], n, at(dc=1)))
        n += 1

    forward(lo, y)
    forward(hi, z)

    def regroup(s, carry):
        for c in range(2):
            piece = spread[pl.ds(s * 2 + c, ROWS, stride=PITCH), :]
            rows[s, :, c * LANES:(c + 1) * LANES] = piece.astype(jnp.bfloat16)
        return carry

    lax.fori_loop(0, NY * NZ * NCORE, regroup, 0)

    order = []
    for k in range(1, NY):
        order.append((lo, *second_lo[k - 1]))
        if k % 2 == 0:
            order.append((hi, *second_hi[k // 2 - 1]))
    for ref, index, number, peer in order:
        remote(ref.at[core, index], ref.at[core, index], number, peer).wait_recv()
        forward(ref, index)
    for copy in forwards:
        copy.wait_recv()

    def contract(t, total):
        for s in range(NZ * NCORE):
            zz, cc = s // NCORE, s % NCORE
            block = jnp.concatenate([lo[cc, t, zz], hi[cc, zz, t]], axis=0)
            total = total + lax.dot_general(
                block, rows[t * (NZ * NCORE) + s], NT, preferred_element_type=jnp.float32
            )
        return total

    total = lax.fori_loop(0, NY, contract, jnp.zeros((WIDTH, ROWS), jnp.float32))

    over_x[x] = jnp.zeros((WIDTH, LANES), jnp.float32)
    over_x[x, :, :ROWS] = total * (0.5 * sign)
    arrivals = []
    for k in range(1, NX):
        copy = remote(over_x.at[x], over_x.at[x], n, at(dx=k))
        copy.start()
        sends.append(copy)
        arrivals.append(remote(over_x.at[x], over_x.at[(x - k + NX) % NX], n, at(dx=k)))
        n += 1
    for copy in arrivals:
        copy.wait_recv()
    total = over_x[0]
    for k in range(1, NX):
        total = total + over_x[k]
    mine = mirror * NH + half
    over_m[mine] = total
    arrivals = []
    for m, h in ((0, 1), (1, 0), (1, 1)):
        peer = at(dy=m * (NY // 2), dh=h)
        theirs = ((mirror + m) % 2) * NH + (half + h) % NH
        copy = remote(over_m.at[mine], over_m.at[mine], n, peer)
        copy.start()
        sends.append(copy)
        arrivals.append(remote(over_m.at[mine], over_m.at[theirs], n, peer))
        n += 1
    for copy in arrivals:
        copy.wait_recv()
    total = (over_m[0] + over_m[1]) + (over_m[2] + over_m[3])

    full = lax.dot_general(
        total, pick, TN, preferred_element_type=jnp.float32, precision=lax.Precision.HIGHEST
    )
    result[...] = full[:ROWS] * factor[...]
    for r in range(ROWS):
        q = r % (OB * OB)
        source = r + mirror * ((q % OB) * OB + q // OB - q)
        out[r:r + 1, :] = result[pl.ds(source, 1), :]
    for copy in sends:
        copy.wait_send()


N_COPIES = 10 + 10 + 12 + 7 + 3


def one_pass(chunk, collective_id, arrays):
    smem = pl.BlockSpec(memory_space=pltpu.SMEM)
    vmem = pl.BlockSpec(memory_space=pltpu.VMEM)
    return pl.pallas_call(
        kernel,
        out_shape=(
            jax.ShapeDtypeStruct((ROWS, LANES), jnp.float32),
            jax.ShapeDtypeStruct((8, LANES), jnp.int32),
        ),
        in_specs=[smem] * 5 + [pl.BlockSpec(memory_space=pl.ANY)] + [vmem] * 5,
        out_specs=(vmem, vmem),
        scratch_shapes=[
            pltpu.VMEM((ROWS, LANES, LANES), jnp.bfloat16),
            pltpu.VMEM((ROWS * PITCH, LANES), jnp.float32),
            pltpu.VMEM((NY * NZ * NCORE, ROWS, 2 * LANES), jnp.bfloat16),
            pltpu.VMEM((NCORE, NY, NZ, HALF, 2 * LANES), jnp.bfloat16),
            pltpu.VMEM((NCORE, NZ, NY, HALF, 2 * LANES), jnp.bfloat16),
            pltpu.VMEM((ROWS, LANES), jnp.float32),
            pltpu.VMEM((NX, WIDTH, LANES), jnp.float32),
            pltpu.VMEM((2 * NH, WIDTH, LANES), jnp.float32),
            pltpu.VMEM((ROWS, LANES), jnp.float32),
            pltpu.SemaphoreType.DMA,
            pltpu.SemaphoreType.DMA((N_COPIES,)),
            pltpu.SemaphoreType.DMA((N_COPIES,)),
        ],
        compiler_params=pltpu.CompilerParams(
            collective_id=collective_id, has_side_effects=True, vmem_limit_bytes=56 * 2**20
        ),
        cost_estimate=pl.CostEstimate(
            flops=2 * ROWS * WIDTH * LANES * LANES, bytes_accessed=2 * ROWS * LANES * LANES, transcendentals=0
        ),
        name="ladder",
    )(*arrays[:4], chunk, *arrays[4:])


def on_device(
    amplitudes, integrals, tile_blocks, occ_irrep, slab_irrep, virt_irrep, ab_irrep, occ_energy, ab_energy
):
    row = lambda vector: vector.reshape(1, LANES)
    arrays = (
        tile_blocks, occ_irrep, slab_irrep, occ_energy,
        amplitudes.reshape(ROWS, LANES, LANES), integrals,
        row(virt_irrep), row(slab_irrep), row(ab_irrep), row(ab_energy),
    )
    update, top = one_pass(jnp.zeros((1,), jnp.int32), 0, arrays)
    last = top[0, 0]

    def again(state):
        chunk, so_far = state
        more, _ = one_pass(chunk.reshape(1), 1, arrays)
        return chunk + 1, so_far + more

    _, update = lax.while_loop(lambda state: state[0] * WIDTH <= last, again, (jnp.int32(1), update))
    return update.reshape(TILES, OB * OB, LANES)


def solution(mesh):
    return jax.shard_map(
        on_device,
        mesh=mesh,
        in_specs=(
            P("pair", None, None, "virt"), P("pair", "virt", None), P("pair", None),
            P(), P(), P("virt"), P(), P(), P(),
        ),
        out_specs=P("pair", None, None),
        check_vma=False,
    )
```

```python
import functools

import jax
import jax.numpy as jnp
from jax import lax
from jax.experimental import pallas as pl
from jax.experimental.pallas import tpu as pltpu
from jax.sharding import PartitionSpec as P

OB = 4
TILES = 6
ROWS = TILES * OB * OB
LANES = 128
WIDTH = 32
HALF = WIDTH // 2
NY, NZ, NCORE, NX, NH = 8, 4, 2, 8, 2
PITCH = 136
FAR_FIRST = (4, 3, 5, 2, 6, 1, 7)
NEAR_FIRST = FAR_FIRST[::-1]
MESH = pl.DeviceIdType.MESH
NT = (((1,), (1,)), ((), ()))
TN = (((0,), (0,)), ((), ()))


def place():
    pair, virt = lax.axis_index("pair"), lax.axis_index("virt")
    return pair // (NZ * NCORE), (pair // NCORE) % NZ, pair % NCORE, virt // NX, virt % NX


def kernel(
    tile_blocks_in, occ_irrep_in, slab_in, occ_energy_in, amps, ints_in, virt_in, slab_row_in, ab_in, ab_energy_in,
    *refs,
):
    chunk_in = refs[0] if len(refs) == 26 else None
    (
        out, top, tile_blocks, occ_irrep, slab_scalar, occ_energy, ints, virt, slab, ab, ab_energy, chunk,
        held, spread, rows, lo, hi, factor, over_x, over_m, result, sem_in, send, recv, ready,
    ) = refs[-25:]
    y, z, core, half, x = place()
    mirror = y // (NY // 2)

    def at(dy=0, dz=0, dc=0, dh=0, dx=0):
        pair = ((y + dy) % NY) * (NZ * NCORE) + ((z + dz) % NZ) * NCORE + (core + dc) % NCORE
        return pair, ((half + dh) % NH) * NX + (x + dx) % NX

    peers = [at(dy=k) for k in FAR_FIRST] + [at(dh=1)] + [at(dx=k) for k in FAR_FIRST]
    peers += [at(dz=k) for k in range(1, NZ)] + [at(dc=1)]
    barrier = pltpu.get_barrier_semaphore()
    for peer in peers:
        pl.semaphore_signal(barrier, inc=1, device_id=peer, device_id_type=MESH)

    loads = []
    for source, target in (
        (ab_in, ab), (virt_in, virt), (slab_in, slab_scalar), (ints_in, ints),
        (tile_blocks_in, tile_blocks), (occ_irrep_in, occ_irrep), (occ_energy_in, occ_energy),
        (slab_row_in, slab), (ab_energy_in, ab_energy), (amps, held), (chunk_in, chunk),
    ):
        if source is None:
            continue
        copy = pltpu.make_async_copy(source, target, sem_in.at[len(loads)])
        copy.start()
        loads.append(copy)
    for copy in loads[:4] + loads[10:]:
        copy.wait()

    def remote(src, dst, number, peer):
        return pltpu.make_async_remote_copy(
            src_ref=src, dst_ref=dst, send_sem=send.at[number], recv_sem=recv.at[number],
            device_id=peer, device_id_type=MESH,
        )

    ab_row = ab[...].reshape(1, LANES)
    ab_rows = jnp.broadcast_to(ab_row, (LANES, LANES))
    ab_cols = jnp.transpose(ab_rows)
    before = lax.broadcasted_iota(jnp.int32, (LANES, LANES), 0) < lax.broadcasted_iota(jnp.int32, (LANES, LANES), 1)
    same = jnp.where((ab_rows == ab_cols) & before, 1.0, 0.0)
    rank = jnp.sum(same, axis=0, keepdims=True).astype(jnp.int32)
    top[0] = jnp.max(rank)
    slot = lax.broadcasted_iota(jnp.int32, (WIDTH, LANES), 0)
    if chunk_in is not None:
        slot = slot + chunk[...] * WIDTH
    pick = jnp.where(slot == jnp.broadcast_to(rank, (WIDTH, LANES)), 1.0, 0.0)
    pick_narrow = pick.astype(jnp.bfloat16)
    virt_rows = jnp.broadcast_to(virt[...], (LANES, LANES))
    virt_cols = jnp.transpose(virt_rows)
    labels = jnp.bitwise_xor(virt_cols, ab_rows)
    own = (y * NZ + z) * NCORE + core
    for c in range(2):
        kept = jnp.where(labels == slab_scalar[own * 2 + c], ints[c].astype(jnp.float32), 0.0).astype(jnp.bfloat16)
        packed = lax.dot_general(pick_narrow, kept, NT, preferred_element_type=jnp.float32).astype(jnp.bfloat16)
        lo[core, y, z, :, c * LANES:(c + 1) * LANES] = packed[:HALF]
        hi[core, z, y, :, c * LANES:(c + 1) * LANES] = packed[HALF:]

    pl.semaphore_wait(barrier, len(peers))
    pl.semaphore_signal(ready, inc=1, device_id=at(dy=NY // 2), device_id_type=MESH)

    sends = []

    def push(ref, peer):
        number = len(sends)
        copy = remote(ref, ref, number, peer)
        copy.start()
        sends.append(copy)
        return lambda arriving: remote(arriving, arriving, number, peer).wait_recv()

    first_lo = {k: push(lo.at[core, y, z], at(dz=k)) for k in range(1, NZ)}
    first_hi = {k: push(hi.at[core, z, y], at(dy=k)) for k in FAR_FIRST}

    for copy in loads[4:10]:
        copy.wait()
    cd = jnp.bitwise_xor(jnp.transpose(jnp.broadcast_to(slab[...], (LANES, LANES))), virt_rows)
    sign = (1 - 2 * mirror).astype(jnp.float32)

    def mask_tile(k, carry):
        for q in range(OB * OB):
            i, j = q // OB, q % OB
            source = k * (OB * OB) + q + mirror * (j * OB + i - q)
            a = tile_blocks[0, k] * OB + (i + mirror * (j - i))
            b = tile_blocks[1, k] * OB + (j + mirror * (i - j))
            irrep = jnp.bitwise_xor(occ_irrep[a], occ_irrep[b])
            energy = occ_energy[a] + occ_energy[b]
            row = k * (OB * OB) + q
            spread[pl.ds(pl.multiple_of(row * PITCH, 8), LANES), :] = jnp.where(
                cd == irrep, held[source].astype(jnp.float32), 0.0
            )
            factor[pl.ds(row, 1), :] = jnp.where(ab_row == irrep, sign / (energy - ab_energy[...]), 0.0)
        return carry

    lax.fori_loop(0, TILES, mask_tile, 0)

    for k, arrived in first_lo.items():
        arrived(lo.at[core, y, (z - k + NZ) % NZ])
    second_lo = {k: push(lo.at[core, y], at(dy=k)) for k in FAR_FIRST}
    for k, arrived in first_hi.items():
        arrived(hi.at[core, z, (y - k + NY) % NY])
    second_hi = {k: push(hi.at[core, z], at(dz=k)) for k in range(1, NZ)}
    sibling_lo = {0: push(lo.at[core, y], at(dc=1))}
    sibling_hi = {0: push(hi.at[core, z], at(dc=1))}

    def regroup(s, carry):
        for c in range(2):
            piece = spread[pl.ds(s * 2 + c, ROWS, stride=PITCH), :]
            rows[s, :, c * LANES:(c + 1) * LANES] = piece.astype(jnp.bfloat16)
        return carry

    lax.fori_loop(0, NY * NZ * NCORE, regroup, 0)

    def contract(total, c, slab_y):
        for zz in range(NZ):
            block = jnp.concatenate([lo[c, slab_y, zz], hi[c, zz, slab_y]], axis=0)
            total = total + lax.dot_general(
                block, rows[(slab_y * NZ + zz) * NCORE + c], NT, preferred_element_type=jnp.float32
            )
        return total

    for k, arrived in second_hi.items():
        source = hi.at[core, (z - k + NZ) % NZ]
        arrived(source)
        sibling_hi[k] = push(source, at(dc=1))
    total = contract(jnp.zeros((WIDTH, ROWS), jnp.float32), core, y)
    for k in NEAR_FIRST:
        slab_y = (y - k + NY) % NY
        source = lo.at[core, slab_y]
        second_lo[k](source)
        sibling_lo[k] = push(source, at(dc=1))
        total = contract(total, core, slab_y)
    for k, arrived in sibling_hi.items():
        arrived(hi.at[1 - core, (z - k + NZ) % NZ])
    for k, arrived in sibling_lo.items():
        slab_y = (y - k + NY) % NY
        arrived(lo.at[1 - core, slab_y])
        total = contract(total, 1 - core, slab_y)

    over_x[x] = jnp.zeros((WIDTH, LANES), jnp.float32)
    over_x[x, :, :ROWS] = total * (0.5 * sign)
    arrivals = {k: push(over_x.at[x], at(dx=k)) for k in FAR_FIRST}
    for k, arrived in arrivals.items():
        arrived(over_x.at[(x - k + NX) % NX])
    total = over_x[0]
    for k in range(1, NX):
        total = total + over_x[k]
    mine = mirror * NH + half
    over_m[mine] = total
    pl.semaphore_wait(ready, 1)
    arrivals = {
        (m, h): push(over_m.at[mine], at(dy=m * (NY // 2), dh=h)) for m, h in ((1, 1), (0, 1), (1, 0))
    }
    for (m, h), arrived in arrivals.items():
        arrived(over_m.at[((mirror + m) % 2) * NH + (half + h) % NH])
    total = (over_m[0] + over_m[1]) + (over_m[2] + over_m[3])

    full = lax.dot_general(
        total, pick, TN, preferred_element_type=jnp.float32, precision=lax.Precision.HIGHEST
    )
    result[...] = full[:ROWS] * factor[...]
    for r in range(ROWS):
        q = r % (OB * OB)
        source = r + mirror * ((q % OB) * OB + q // OB - q)
        out[r:r + 1, :] = result[pl.ds(source, 1), :]
    for copy in sends:
        copy.wait_send()


N_COPIES = 10 + 10 + 12 + 7 + 3


def one_pass(collective_id, arrays):
    smem = pl.BlockSpec(memory_space=pltpu.SMEM)
    vmem = pl.BlockSpec(memory_space=pltpu.VMEM)
    return pl.pallas_call(
        kernel,
        out_shape=(
            jax.ShapeDtypeStruct((ROWS, LANES), jnp.float32),
            jax.ShapeDtypeStruct((1,), jnp.int32),
        ),
        in_specs=[pl.BlockSpec(memory_space=pl.ANY)] * len(arrays),
        out_specs=(vmem, smem),
        scratch_shapes=[
            pltpu.SMEM((2, TILES), jnp.int32),
            pltpu.SMEM((LANES,), jnp.int32),
            pltpu.SMEM((LANES,), jnp.int32),
            pltpu.SMEM((LANES,), jnp.float32),
            pltpu.VMEM((2, LANES, LANES), jnp.bfloat16),
            pltpu.VMEM((1, LANES), jnp.int32),
            pltpu.VMEM((1, LANES), jnp.int32),
            pltpu.VMEM((1, LANES), jnp.int32),
            pltpu.VMEM((1, LANES), jnp.float32),
            pltpu.VMEM((1, LANES), jnp.int32),
            pltpu.VMEM((ROWS, LANES, LANES), jnp.bfloat16),
            pltpu.VMEM((ROWS * PITCH, LANES), jnp.float32),
            pltpu.VMEM((NY * NZ * NCORE, ROWS, 2 * LANES), jnp.bfloat16),
            pltpu.VMEM((NCORE, NY, NZ, HALF, 2 * LANES), jnp.bfloat16),
            pltpu.VMEM((NCORE, NZ, NY, HALF, 2 * LANES), jnp.bfloat16),
            pltpu.VMEM((ROWS, LANES), jnp.float32),
            pltpu.VMEM((NX, WIDTH, LANES), jnp.float32),
            pltpu.VMEM((2 * NH, WIDTH, LANES), jnp.float32),
            pltpu.VMEM((ROWS, LANES), jnp.float32),
            pltpu.SemaphoreType.DMA((11,)),
            pltpu.SemaphoreType.DMA((N_COPIES,)),
            pltpu.SemaphoreType.DMA((N_COPIES,)),
            pltpu.SemaphoreType.REGULAR,
        ],
        compiler_params=pltpu.CompilerParams(
            collective_id=collective_id, has_side_effects=True, vmem_limit_bytes=56 * 2**20
        ),
        cost_estimate=pl.CostEstimate(
            flops=2 * ROWS * WIDTH * LANES * LANES, bytes_accessed=2 * ROWS * LANES * LANES, transcendentals=0
        ),
        name="ladder",
    )(*arrays)


def on_device(
    amplitudes, integrals, tile_blocks, occ_irrep, slab_irrep, virt_irrep, ab_irrep, occ_energy, ab_energy
):
    row = lambda vector: vector.reshape(1, LANES)
    arrays = (
        tile_blocks.T, occ_irrep, slab_irrep, occ_energy,
        amplitudes.reshape(ROWS, LANES, LANES), integrals, row(virt_irrep), row(slab_irrep),
        row(ab_irrep), row(ab_energy),
    )
    update, top = one_pass(0, arrays)

    def again(state):
        chunk, so_far = state
        more, _ = one_pass(1, (*arrays, jnp.full((1, LANES), chunk)))
        return chunk + 1, so_far + more

    _, update = lax.while_loop(lambda state: state[0] * WIDTH <= top[0], again, (jnp.int32(1), update))
    return update.reshape(TILES, OB * OB, LANES)


def solution(mesh):
    return jax.shard_map(
        on_device,
        mesh=mesh,
        in_specs=(
            P("pair", None, None, "virt"), P("pair", "virt", None), P("pair", None),
            P(), P(), P("virt"), P(), P(), P(),
        ),
        out_specs=P("pair", None, None),
        check_vma=False,
    )
```

```python
import functools

import jax
import jax.numpy as jnp
from jax import lax
from jax.experimental import pallas as pl
from jax.experimental.pallas import tpu as pltpu
from jax.sharding import PartitionSpec as P

OB = 4
TILES = 6
ROWS = TILES * OB * OB
LANES = 128
WIDTH = 32
HALF = WIDTH // 2
NY, NZ, NCORE, NX, NH = 8, 4, 2, 8, 2
PITCH = 136
FAR_FIRST = (4, 3, 5, 2, 6, 1, 7)
NEAR_FIRST = FAR_FIRST[::-1]
MESH = pl.DeviceIdType.MESH
NT = (((1,), (1,)), ((), ()))
TN = (((0,), (0,)), ((), ()))


def place():
    pair, virt = lax.axis_index("pair"), lax.axis_index("virt")
    return pair // (NZ * NCORE), (pair // NCORE) % NZ, pair % NCORE, virt // NX, virt % NX


def kernel(
    tile_blocks_in, occ_irrep_in, slab_in, occ_energy_in, amps, ints_in, virt_in, slab_row_in, ab_in, ab_energy_in,
    *refs,
):
    chunk_in = refs[0] if len(refs) == 27 else None
    (
        out, top, tile_blocks, occ_irrep, slab_scalar, occ_energy, ints, virt, slab, ab, ab_energy, chunk,
        held, spread, rows, blocks, factor, over_x, over_m, result, sem_in, send, recv, ready, across, above,
    ) = refs[-26:]
    y, z, core, half, x = place()
    mirror = y // (NY // 2)

    def at(dy=0, dz=0, dc=0, dh=0, dx=0):
        pair = ((y + dy) % NY) * (NZ * NCORE) + ((z + dz + NZ) % NZ) * NCORE + (core + dc) % NCORE
        return pair, ((half + dh) % NH) * NX + (x + dx) % NX

    peers = [at(dy=k) for k in FAR_FIRST] + [at(dx=k) for k in FAR_FIRST] + [at(dc=1)]
    barrier = pltpu.get_barrier_semaphore()
    for peer in peers:
        pl.semaphore_signal(barrier, inc=1, device_id=peer, device_id_type=MESH)
    for k in range(1, NZ):
        @pl.when(z + k < NZ)
        def _():
            pl.semaphore_signal(barrier, inc=1, device_id=at(dz=k), device_id_type=MESH)

    @pl.when(half == 0)
    def _():
        pl.semaphore_signal(barrier, inc=1, device_id=at(dh=1), device_id_type=MESH)

    loads = []
    for source, target in (
        (ab_in, ab), (virt_in, virt), (slab_in, slab_scalar), (ints_in, ints),
        (tile_blocks_in, tile_blocks), (occ_irrep_in, occ_irrep), (occ_energy_in, occ_energy),
        (slab_row_in, slab), (ab_energy_in, ab_energy), (amps, held), (chunk_in, chunk),
    ):
        if source is None:
            continue
        copy = pltpu.make_async_copy(source, target, sem_in.at[len(loads)])
        copy.start()
        loads.append(copy)
    for copy in loads[:4] + loads[10:]:
        copy.wait()

    def remote(src, dst, number, peer):
        return pltpu.make_async_remote_copy(
            src_ref=src, dst_ref=dst, send_sem=send.at[number], recv_sem=recv.at[number],
            device_id=peer, device_id_type=MESH,
        )

    ab_row = ab[...].reshape(1, LANES)
    ab_rows = jnp.broadcast_to(ab_row, (LANES, LANES))
    ab_cols = jnp.transpose(ab_rows)
    before = lax.broadcasted_iota(jnp.int32, (LANES, LANES), 0) < lax.broadcasted_iota(jnp.int32, (LANES, LANES), 1)
    same = jnp.where((ab_rows == ab_cols) & before, 1.0, 0.0)
    rank = jnp.sum(same, axis=0, keepdims=True).astype(jnp.int32)
    top[0] = jnp.max(rank)
    slot = lax.broadcasted_iota(jnp.int32, (WIDTH, LANES), 0)
    if chunk_in is not None:
        slot = slot + chunk[...] * WIDTH
    pick = jnp.where(slot == jnp.broadcast_to(rank, (WIDTH, LANES)), 1.0, 0.0)
    pick_narrow = pick.astype(jnp.bfloat16)
    virt_rows = jnp.broadcast_to(virt[...], (LANES, LANES))
    virt_cols = jnp.transpose(virt_rows)
    labels = jnp.bitwise_xor(virt_cols, ab_rows)
    own = (y * NZ + z) * NCORE + core
    for c in range(2):
        kept = jnp.where(labels == slab_scalar[own * 2 + c], ints[c].astype(jnp.float32), 0.0).astype(jnp.bfloat16)
        packed = lax.dot_general(pick_narrow, kept, NT, preferred_element_type=jnp.float32).astype(jnp.bfloat16)
        for h in range(2):
            blocks[core, 0, 0, h, :, c * LANES:(c + 1) * LANES] = packed[h * HALF:(h + 1) * HALF]

    pl.semaphore_wait(barrier, len(peers) + z + half)
    for k in range(1, NZ):
        @pl.when(z >= k)
        def _():
            pl.semaphore_signal(above.at[k], inc=1, device_id=at(dz=-k), device_id_type=MESH)

    def ready_for_mirror():
        pl.semaphore_signal(ready, inc=1, device_id=at(dy=NY // 2), device_id_type=MESH)

    @pl.when(half == 1)
    def _():
        pl.semaphore_signal(across, inc=1, device_id=at(dh=1), device_id_type=MESH)
        ready_for_mirror()

    sends = []

    def push(source, target, peer, start=True):
        copy = remote(source, target, len(sends), peer)
        if start:
            copy.start()
        sends.append(copy)
        return copy

    own_block = blocks.at[core, 0, 0]
    near_z = {k: push(own_block, blocks.at[core, 0, k], at(dz=k), start=False) for k in range(1, NZ)}
    for k, copy in near_z.items():
        @pl.when(z + k >= NZ)
        def _():
            copy.start()

    near_y = [push(own_block, blocks.at[core, k, 0], at(dy=k)) for k in FAR_FIRST]

    for copy in loads[4:10]:
        copy.wait()
    cd = jnp.bitwise_xor(jnp.transpose(jnp.broadcast_to(slab[...], (LANES, LANES))), virt_rows)
    sign = (1 - 2 * mirror).astype(jnp.float32)

    def mask_tile(k, carry):
        for q in range(OB * OB):
            i, j = q // OB, q % OB
            source = k * (OB * OB) + q + mirror * (j * OB + i - q)
            a = tile_blocks[0, k] * OB + (i + mirror * (j - i))
            b = tile_blocks[1, k] * OB + (j + mirror * (i - j))
            irrep = jnp.bitwise_xor(occ_irrep[a], occ_irrep[b])
            energy = occ_energy[a] + occ_energy[b]
            row = k * (OB * OB) + q
            spread[pl.ds(pl.multiple_of(row * PITCH, 8), LANES), :] = jnp.where(
                cd == irrep, held[source].astype(jnp.float32), 0.0
            )
            factor[pl.ds(row, 1), :] = jnp.where(ab_row == irrep, sign / (energy - ab_energy[...]), 0.0)
        return carry

    lax.fori_loop(0, TILES, mask_tile, 0)

    def regroup(s, carry):
        for c in range(2):
            piece = spread[pl.ds(s * 2 + c, ROWS, stride=PITCH), :]
            rows[s, :, c * LANES:(c + 1) * LANES] = piece.astype(jnp.bfloat16)
        return carry

    lax.fori_loop(0, NY * NZ * NCORE, regroup, 0)

    for k, copy in near_z.items():
        @pl.when(z + k < NZ)
        def _():
            pl.semaphore_wait(above.at[k], 1)
            copy.start()

    for copy in near_z.values():
        copy.wait_recv()
    far_lo = {
        k: push(blocks.at[core, 0, pl.ds(1, NZ - 1), 0], blocks.at[core, k, pl.ds(1, NZ - 1), 0], at(dy=k))
        for k in FAR_FIRST
    }
    for copy in near_y:
        copy.wait_recv()
    far_hi = {
        k: push(blocks.at[core, pl.ds(1, NY - 1), 0, 1], blocks.at[core, pl.ds(1, NY - 1), k, 1], at(dz=k))
        for k in range(1, NZ)
    }

    def share(part):
        return push(part, part, at(dc=1))

    shared = [share(blocks.at[core, :, 0]), share(blocks.at[core, 0, pl.ds(1, NZ - 1)])]

    def contract(total, c, ky, kzs):
        for kz in kzs:
            source = ((y - ky + NY) % NY * NZ + (z - kz + NZ) % NZ) * NCORE + c
            total = total + lax.dot_general(
                blocks[c, ky, kz].reshape(WIDTH, 2 * LANES), rows[source], NT, preferred_element_type=jnp.float32
            )
        return total

    def contract_near(total, c):
        total = contract(total, c, 0, range(NZ))
        for ky in range(1, NY):
            total = contract(total, c, ky, range(1))
        return total

    total = contract_near(jnp.zeros((WIDTH, ROWS), jnp.float32), core)
    for copy in shared:
        copy.wait_recv()
    total = contract_near(total, 1 - core)
    shared_hi, shared_lo = [], []
    for k, copy in far_hi.items():
        copy.wait_recv()
        shared_hi.append(share(blocks.at[core, pl.ds(1, NY - 1), k, 1]))
    for k in NEAR_FIRST:
        far_lo[k].wait_recv()
        shared_lo.append(share(blocks.at[core, k, pl.ds(1, NZ - 1), 0]))
    for k in NEAR_FIRST:
        total = contract(total, core, k, range(1, NZ))
    for copy in shared_hi:
        copy.wait_recv()
    for k, copy in zip(NEAR_FIRST, shared_lo):
        copy.wait_recv()
        total = contract(total, 1 - core, k, range(1, NZ))

    @pl.when(half == 0)
    def _():
        pl.semaphore_wait(across, 1)
        ready_for_mirror()

    over_x[x] = jnp.zeros((WIDTH, LANES), jnp.float32)
    over_x[x, :, :ROWS] = total * (0.5 * sign)
    arrivals = [push(over_x.at[x], over_x.at[x], at(dx=k)) for k in FAR_FIRST]
    for copy in arrivals:
        copy.wait_recv()
    total = over_x[0]
    for k in range(1, NX):
        total = total + over_x[k]
    mine = mirror * NH + half
    over_m[mine] = total
    pl.semaphore_wait(ready, 1)
    arrivals = [
        push(over_m.at[mine], over_m.at[mine], at(dy=m * (NY // 2), dh=h)) for m, h in ((1, 1), (0, 1), (1, 0))
    ]
    for copy in arrivals:
        copy.wait_recv()
    total = (over_m[0] + over_m[1]) + (over_m[2] + over_m[3])

    full = lax.dot_general(
        total, pick, TN, preferred_element_type=jnp.float32, precision=lax.Precision.HIGHEST
    )
    scaled = full[:ROWS] * factor[...]

    @pl.when(mirror == 0)
    def _():
        out[...] = scaled

    @pl.when(mirror == 1)
    def _():
        result[...] = scaled
        for r in range(ROWS):
            q = r % (OB * OB)
            source = r + (q % OB) * OB + q // OB - q
            out[r:r + 1, :] = result[source:source + 1, :]

    for copy in sends:
        copy.wait_send()


N_COPIES = 10 + 10 + 12 + 7 + 3


def one_pass(collective_id, arrays):
    smem = pl.BlockSpec(memory_space=pltpu.SMEM)
    vmem = pl.BlockSpec(memory_space=pltpu.VMEM)
    return pl.pallas_call(
        kernel,
        out_shape=(
            jax.ShapeDtypeStruct((ROWS, LANES), jnp.float32),
            jax.ShapeDtypeStruct((1,), jnp.int32),
        ),
        in_specs=[pl.BlockSpec(memory_space=pl.ANY)] * len(arrays),
        out_specs=(vmem, smem),
        scratch_shapes=[
            pltpu.SMEM((2, TILES), jnp.int32),
            pltpu.SMEM((LANES,), jnp.int32),
            pltpu.SMEM((LANES,), jnp.int32),
            pltpu.SMEM((LANES,), jnp.float32),
            pltpu.VMEM((2, LANES, LANES), jnp.bfloat16),
            pltpu.VMEM((1, LANES), jnp.int32),
            pltpu.VMEM((1, LANES), jnp.int32),
            pltpu.VMEM((1, LANES), jnp.int32),
            pltpu.VMEM((1, LANES), jnp.float32),
            pltpu.VMEM((1, LANES), jnp.int32),
            pltpu.VMEM((ROWS, LANES, LANES), jnp.bfloat16),
            pltpu.VMEM((ROWS * PITCH, LANES), jnp.float32),
            pltpu.VMEM((NY * NZ * NCORE, ROWS, 2 * LANES), jnp.bfloat16),
            pltpu.VMEM((NCORE, NY, NZ, 2, HALF, 2 * LANES), jnp.bfloat16),
            pltpu.VMEM((ROWS, LANES), jnp.float32),
            pltpu.VMEM((NX, WIDTH, LANES), jnp.float32),
            pltpu.VMEM((2 * NH, WIDTH, LANES), jnp.float32),
            pltpu.VMEM((ROWS, LANES), jnp.float32),
            pltpu.SemaphoreType.DMA((11,)),
            pltpu.SemaphoreType.DMA((N_COPIES,)),
            pltpu.SemaphoreType.DMA((N_COPIES,)),
            pltpu.SemaphoreType.REGULAR,
            pltpu.SemaphoreType.REGULAR,
            pltpu.SemaphoreType.REGULAR((NZ,)),
        ],
        compiler_params=pltpu.CompilerParams(
            collective_id=collective_id, has_side_effects=True, vmem_limit_bytes=56 * 2**20
        ),
        cost_estimate=pl.CostEstimate(
            flops=2 * ROWS * WIDTH * LANES * LANES, bytes_accessed=2 * ROWS * LANES * LANES, transcendentals=0
        ),
        name="ladder",
    )(*arrays)


def on_device(
    amplitudes, integrals, tile_blocks, occ_irrep, slab_irrep, virt_irrep, ab_irrep, occ_energy, ab_energy
):
    row = lambda vector: vector.reshape(1, LANES)
    arrays = (
        tile_blocks.T, occ_irrep, slab_irrep, occ_energy,
        amplitudes.reshape(ROWS, LANES, LANES), integrals, row(virt_irrep), row(slab_irrep),
        row(ab_irrep), row(ab_energy),
    )
    update, top = one_pass(0, arrays)

    def again(state):
        chunk, so_far = state
        more, _ = one_pass(1, (*arrays, jnp.full((1, LANES), chunk)))
        return chunk + 1, so_far + more

    _, update = lax.while_loop(lambda state: state[0] * WIDTH <= top[0], again, (jnp.int32(1), update))
    return update.reshape(TILES, OB * OB, LANES)


def solution(mesh):
    return jax.shard_map(
        on_device,
        mesh=mesh,
        in_specs=(
            P("pair", None, None, "virt"), P("pair", "virt", None), P("pair", None),
            P(), P(), P("virt"), P(), P(), P(),
        ),
        out_specs=P("pair", None, None),
        check_vma=False,
    )
```

```python
import functools

import jax
import jax.numpy as jnp
from jax import lax
from jax.experimental import pallas as pl
from jax.experimental.pallas import tpu as pltpu
from jax.sharding import PartitionSpec as P

OB = 4
TILES = 6
ROWS = TILES * OB * OB
LANES = 128
WIDTH = 32
HALF = WIDTH // 2
NY, NZ, NCORE, NX, NH = 8, 4, 2, 8, 2
PITCH = 136
FAR_FIRST = (4, 3, 5, 2, 6, 1, 7)
NEAR_FIRST = FAR_FIRST[::-1]
MESH = pl.DeviceIdType.MESH
NT = (((1,), (1,)), ((), ()))
TN = (((0,), (0,)), ((), ()))


def place():
    pair, virt = lax.axis_index("pair"), lax.axis_index("virt")
    return pair // (NZ * NCORE), (pair // NCORE) % NZ, pair % NCORE, virt // NX, virt % NX


def kernel(
    tile_blocks_in, occ_irrep_in, slab_in, occ_energy_in, amps, ints_in, virt_in, slab_row_in, ab_in, ab_energy_in,
    *refs,
):
    chunk_in = refs[0] if len(refs) == 27 else None
    (
        out, top, tile_blocks, occ_irrep, slab_scalar, occ_energy, ints, virt, slab, ab, ab_energy, chunk,
        held, spread, rows, blocks, factor, over_x, over_m, result, sem_in, send, recv, ready, across, above,
    ) = refs[-26:]
    y, z, core, half, x = place()
    mirror = y // (NY // 2)

    def at(dy=0, dz=0, dc=0, dh=0, dx=0):
        pair = ((y + dy) % NY) * (NZ * NCORE) + ((z + dz + NZ) % NZ) * NCORE + (core + dc) % NCORE
        return pair, ((half + dh) % NH) * NX + (x + dx) % NX

    peers = [at(dy=k) for k in FAR_FIRST] + [at(dx=k) for k in FAR_FIRST] + [at(dc=1)]
    barrier = pltpu.get_barrier_semaphore()
    for peer in peers:
        pl.semaphore_signal(barrier, inc=1, device_id=peer, device_id_type=MESH)
    for k in range(1, NZ):
        @pl.when(z + k < NZ)
        def _():
            pl.semaphore_signal(barrier, inc=1, device_id=at(dz=k), device_id_type=MESH)

    @pl.when(half == 0)
    def _():
        pl.semaphore_signal(barrier, inc=1, device_id=at(dh=1), device_id_type=MESH)

    loads = []
    for source, target in (
        (ab_in, ab), (virt_in, virt), (slab_in, slab_scalar), (ints_in, ints),
        (tile_blocks_in, tile_blocks), (occ_irrep_in, occ_irrep), (occ_energy_in, occ_energy),
        (slab_row_in, slab), (ab_energy_in, ab_energy), (amps, held), (chunk_in, chunk),
    ):
        if source is None:
            continue
        copy = pltpu.make_async_copy(source, target, sem_in.at[len(loads)])
        copy.start()
        loads.append(copy)
    for copy in loads[:4] + loads[10:]:
        copy.wait()

    def remote(src, dst, number, peer):
        return pltpu.make_async_remote_copy(
            src_ref=src, dst_ref=dst, send_sem=send.at[number], recv_sem=recv.at[number],
            device_id=peer, device_id_type=MESH,
        )

    ab_row = ab[...].reshape(1, LANES)
    ab_rows = jnp.broadcast_to(ab_row, (LANES, LANES))
    ab_cols = jnp.transpose(ab_rows)
    before = lax.broadcasted_iota(jnp.int32, (LANES, LANES), 0) < lax.broadcasted_iota(jnp.int32, (LANES, LANES), 1)
    same = jnp.where((ab_rows == ab_cols) & before, 1.0, 0.0)
    rank = jnp.sum(same, axis=0, keepdims=True).astype(jnp.int32)
    top[0] = jnp.max(rank)
    slot = lax.broadcasted_iota(jnp.int32, (WIDTH, LANES), 0)
    if chunk_in is not None:
        slot = slot + chunk[...] * WIDTH
    pick = jnp.where(slot == jnp.broadcast_to(rank, (WIDTH, LANES)), 1.0, 0.0)
    pick_narrow = pick.astype(jnp.bfloat16)
    virt_rows = jnp.broadcast_to(virt[...], (LANES, LANES))
    virt_cols = jnp.transpose(virt_rows)
    labels = jnp.bitwise_xor(virt_cols, ab_rows)
    own = (y * NZ + z) * NCORE + core
    for c in range(2):
        kept = jnp.where(labels == slab_scalar[own * 2 + c], ints[c].astype(jnp.float32), 0.0).astype(jnp.bfloat16)
        packed = lax.dot_general(pick_narrow, kept, NT, preferred_element_type=jnp.float32).astype(jnp.bfloat16)
        for h in range(2):
            blocks[core, 0, 0, h, :, c * LANES:(c + 1) * LANES] = packed[h * HALF:(h + 1) * HALF]

    pl.semaphore_wait(barrier, len(peers) + z + half)
    for k in range(1, NZ):
        @pl.when(z >= k)
        def _():
            pl.semaphore_signal(above.at[k], inc=1, device_id=at(dz=-k), device_id_type=MESH)

    def ready_for_mirror():
        pl.semaphore_signal(ready, inc=1, device_id=at(dy=NY // 2), device_id_type=MESH)

    @pl.when(half == 1)
    def _():
        pl.semaphore_signal(across, inc=1, device_id=at(dh=1), device_id_type=MESH)
        ready_for_mirror()

    sends = []

    def push(source, target, peer, start=True):
        copy = remote(source, target, len(sends), peer)
        if start:
            copy.start()
        sends.append(copy)
        return copy

    own_block = blocks.at[core, 0, 0]
    near_z = {k: push(own_block, blocks.at[core, 0, k], at(dz=k), start=False) for k in range(1, NZ)}
    for k, copy in near_z.items():
        @pl.when(z + k >= NZ)
        def _():
            copy.start()

    near_y = [push(own_block, blocks.at[core, k, 0], at(dy=k)) for k in FAR_FIRST]

    for copy in loads[4:10]:
        copy.wait()
    cd = jnp.bitwise_xor(jnp.transpose(jnp.broadcast_to(slab[...], (LANES, LANES))), virt_rows)
    sign = (1 - 2 * mirror).astype(jnp.float32)

    def mask_tile(k, carry):
        for q in range(OB * OB):
            i, j = q // OB, q % OB
            source = k * (OB * OB) + q + mirror * (j * OB + i - q)
            a = tile_blocks[0, k] * OB + (i + mirror * (j - i))
            b = tile_blocks[1, k] * OB + (j + mirror * (i - j))
            irrep = jnp.bitwise_xor(occ_irrep[a], occ_irrep[b])
            energy = occ_energy[a] + occ_energy[b]
            row = k * (OB * OB) + q
            spread[pl.ds(pl.multiple_of(row * PITCH, 8), LANES), :] = jnp.where(
                cd == irrep, held[source].astype(jnp.float32), 0.0
            )
            factor[pl.ds(row, 1), :] = jnp.where(ab_row == irrep, sign / (energy - ab_energy[...]), 0.0)
        return carry

    lax.fori_loop(0, TILES, mask_tile, 0)

    def regroup(s, carry):
        for c in range(2):
            piece = spread[pl.ds(s * 2 + c, ROWS, stride=PITCH), :]
            rows[s, :, c * LANES:(c + 1) * LANES] = piece.astype(jnp.bfloat16)
        return carry

    lax.fori_loop(0, NY * NZ * NCORE, regroup, 0)

    for k, copy in near_z.items():
        @pl.when(z + k < NZ)
        def _():
            pl.semaphore_wait(above.at[k], 1)
            copy.start()

    for k in (3, 2):
        near_z[k].wait_recv()
    far_lo = {
        k: push(blocks.at[core, 0, pl.ds(2, NZ - 2), 0], blocks.at[core, k, pl.ds(2, NZ - 2), 0], at(dy=k))
        for k in FAR_FIRST
    }
    near_z[1].wait_recv()
    far_one = {k: push(blocks.at[core, 0, 1], blocks.at[core, k, 1], at(dy=k)) for k in FAR_FIRST}
    for copy in near_y:
        copy.wait_recv()
    far_hi = {
        k: push(blocks.at[core, pl.ds(1, NY - 1), 0, 1], blocks.at[core, pl.ds(1, NY - 1), k, 1], at(dz=k))
        for k in range(2, NZ)
    }

    def share(part):
        return push(part, part, at(dc=1))

    shared = [share(blocks.at[core, :, 0]), share(blocks.at[core, 0, pl.ds(1, NZ - 1)])]

    def contract(total, c, ky, kzs):
        for kz in kzs:
            source = ((y - ky + NY) % NY * NZ + (z - kz + NZ) % NZ) * NCORE + c
            total = total + lax.dot_general(
                blocks[c, ky, kz].reshape(WIDTH, 2 * LANES), rows[source], NT, preferred_element_type=jnp.float32
            )
        return total

    def contract_near(total, c):
        total = contract(total, c, 0, range(NZ))
        for ky in range(1, NY):
            total = contract(total, c, ky, range(1))
        return total

    total = contract_near(jnp.zeros((WIDTH, ROWS), jnp.float32), core)
    for copy in shared:
        copy.wait_recv()
    total = contract_near(total, 1 - core)
    shared_hi, shared_lo, shared_one = [], [], []
    for k, copy in far_hi.items():
        copy.wait_recv()
        shared_hi.append(share(blocks.at[core, pl.ds(1, NY - 1), k, 1]))
    for k in NEAR_FIRST:
        far_lo[k].wait_recv()
        shared_lo.append(share(blocks.at[core, k, pl.ds(2, NZ - 2), 0]))
    for k in NEAR_FIRST:
        total = contract(total, core, k, range(2, NZ))
    for k in NEAR_FIRST:
        far_one[k].wait_recv()
        shared_one.append(share(blocks.at[core, k, 1]))
    for copy in shared_hi:
        copy.wait_recv()
    for k, copy in zip(NEAR_FIRST, shared_lo):
        copy.wait_recv()
        total = contract(total, 1 - core, k, range(2, NZ))
    for k in NEAR_FIRST:
        total = contract(total, core, k, range(1, 2))
    for k, copy in zip(NEAR_FIRST, shared_one):
        copy.wait_recv()
        total = contract(total, 1 - core, k, range(1, 2))

    @pl.when(half == 0)
    def _():
        pl.semaphore_wait(across, 1)
        ready_for_mirror()

    over_x[x] = jnp.zeros((WIDTH, LANES), jnp.float32)
    over_x[x, :, :ROWS] = total * (0.5 * sign)
    arrivals = [push(over_x.at[x], over_x.at[x], at(dx=k)) for k in FAR_FIRST]
    for copy in arrivals:
        copy.wait_recv()
    total = over_x[0]
    for k in range(1, NX):
        total = total + over_x[k]
    mine = mirror * NH + half
    over_m[mine] = total
    pl.semaphore_wait(ready, 1)
    arrivals = [
        push(over_m.at[mine], over_m.at[mine], at(dy=m * (NY // 2), dh=h)) for m, h in ((1, 1), (0, 1), (1, 0))
    ]
    for copy in arrivals:
        copy.wait_recv()
    total = (over_m[0] + over_m[1]) + (over_m[2] + over_m[3])

    full = lax.dot_general(
        total, pick, TN, preferred_element_type=jnp.float32, precision=lax.Precision.HIGHEST
    )
    scaled = full[:ROWS] * factor[...]

    @pl.when(mirror == 0)
    def _():
        out[...] = scaled

    @pl.when(mirror == 1)
    def _():
        result[...] = scaled
        for r in range(ROWS):
            q = r % (OB * OB)
            source = r + (q % OB) * OB + q // OB - q
            out[r:r + 1, :] = result[source:source + 1, :]

    for copy in sends:
        copy.wait_send()


N_COPIES = 10 + 16 + 18 + 7 + 3


def one_pass(collective_id, arrays):
    smem = pl.BlockSpec(memory_space=pltpu.SMEM)
    vmem = pl.BlockSpec(memory_space=pltpu.VMEM)
    return pl.pallas_call(
        kernel,
        out_shape=(
            jax.ShapeDtypeStruct((ROWS, LANES), jnp.float32),
            jax.ShapeDtypeStruct((1,), jnp.int32),
        ),
        in_specs=[pl.BlockSpec(memory_space=pl.ANY)] * len(arrays),
        out_specs=(vmem, smem),
        scratch_shapes=[
            pltpu.SMEM((2, TILES), jnp.int32),
            pltpu.SMEM((LANES,), jnp.int32),
            pltpu.SMEM((LANES,), jnp.int32),
            pltpu.SMEM((LANES,), jnp.float32),
            pltpu.VMEM((2, LANES, LANES), jnp.bfloat16),
            pltpu.VMEM((1, LANES), jnp.int32),
            pltpu.VMEM((1, LANES), jnp.int32),
            pltpu.VMEM((1, LANES), jnp.int32),
            pltpu.VMEM((1, LANES), jnp.float32),
            pltpu.VMEM((1, LANES), jnp.int32),
            pltpu.VMEM((ROWS, LANES, LANES), jnp.bfloat16),
            pltpu.VMEM((ROWS * PITCH, LANES), jnp.float32),
            pltpu.VMEM((NY * NZ * NCORE, ROWS, 2 * LANES), jnp.bfloat16),
            pltpu.VMEM((NCORE, NY, NZ, 2, HALF, 2 * LANES), jnp.bfloat16),
            pltpu.VMEM((ROWS, LANES), jnp.float32),
            pltpu.VMEM((NX, WIDTH, LANES), jnp.float32),
            pltpu.VMEM((2 * NH, WIDTH, LANES), jnp.float32),
            pltpu.VMEM((ROWS, LANES), jnp.float32),
            pltpu.SemaphoreType.DMA((11,)),
            pltpu.SemaphoreType.DMA((N_COPIES,)),
            pltpu.SemaphoreType.DMA((N_COPIES,)),
            pltpu.SemaphoreType.REGULAR,
            pltpu.SemaphoreType.REGULAR,
            pltpu.SemaphoreType.REGULAR((NZ,)),
        ],
        compiler_params=pltpu.CompilerParams(
            collective_id=collective_id, has_side_effects=True, vmem_limit_bytes=56 * 2**20
        ),
        cost_estimate=pl.CostEstimate(
            flops=2 * ROWS * WIDTH * LANES * LANES, bytes_accessed=2 * ROWS * LANES * LANES, transcendentals=0
        ),
        name="ladder",
    )(*arrays)


def on_device(
    amplitudes, integrals, tile_blocks, occ_irrep, slab_irrep, virt_irrep, ab_irrep, occ_energy, ab_energy
):
    row = lambda vector: vector.reshape(1, LANES)
    arrays = (
        tile_blocks.T, occ_irrep, slab_irrep, occ_energy,
        amplitudes.reshape(ROWS, LANES, LANES), integrals, row(virt_irrep), row(slab_irrep),
        row(ab_irrep), row(ab_energy),
    )
    update, top = one_pass(0, arrays)

    def again(state):
        chunk, so_far = state
        more, _ = one_pass(1, (*arrays, jnp.full((1, LANES), chunk)))
        return chunk + 1, so_far + more

    _, update = lax.while_loop(lambda state: state[0] * WIDTH <= top[0], again, (jnp.int32(1), update))
    return update.reshape(TILES, OB * OB, LANES)


def solution(mesh):
    return jax.shard_map(
        on_device,
        mesh=mesh,
        in_specs=(
            P("pair", None, None, "virt"), P("pair", "virt", None), P("pair", None),
            P(), P(), P("virt"), P(), P(), P(),
        ),
        out_specs=P("pair", None, None),
        check_vma=False,
    )
```
